32 devices in a mesh: elem: 4 (over y, core), col: 4 (over z), pole: 2 (over x).
Axes of the slice: x: 2, y: 2, z: 4, core: 2. Of those that a mesh axis runs over, the one named last changes fastest.
Arguments:
- basis_seed: bfloat16 [4, 16, 4, 16, 384], P('elem', 'pole', 'col'), may hold values from -6 to 6
- potential: bfloat16 [4, 16, 256], P('elem'), may hold values from 0 to 2
Outputs:
- diag_blocks: float32 [4, 96, 96], P('elem', 'col')
- coupling_blocks: float32 [4, 2, 96, 96], P('elem', None, 'col')
The draws below stay inside these ranges and needn't reach their ends.
All inputs are finite; a program needn't handle non-finite values.
Results may differ from the reference program's by a relative error of at most 0.0041.
Values may be sent and summed in bfloat16 or wider, within the bound.
A program may use at most 64 MiB of HBM per device.

```python
import jax
import jax.numpy as jnp
from jax import lax

NB = 96
C = 12
E = 16
DEG = 4
PASSES = 2
ELEMS = 4
N_COL = 4


def level_of(rng, extent, cuts, smallest, top_value):
    def one(position, parts):
        heights = jax.random.uniform(jax.random.fold_in(jax.random.fold_in(rng, 6), position), (parts,), jnp.float32, smallest / len(cuts), top_value / len(cuts))
        return jnp.repeat(jnp.exp(heights), extent[position] // parts).reshape((-1,) + (1,) * (len(extent) - position - 1))

    factor_of = one(*cuts[0])
    for cut in cuts[1:]:
        factor_of = factor_of * one(*cut)
    return factor_of


def gaussian(own_key, extent, width, limit, shards=(), kind=jnp.bfloat16):
    loudness = level_of(own_key, extent, shards, -0.22, 0.18) if shards else 1.0
    drawn = jax.random.normal(own_key, extent, jnp.float32) * width * loudness
    return jnp.minimum(jnp.maximum(drawn, -limit), limit).astype(kind)


def setup_inputs(seed: int = 0) -> dict:
    arg_keys = jax.random.split(jax.random.key(seed), 3)
    basis_seed = gaussian(arg_keys[0], (ELEMS, E, N_COL, E, E * (NB // N_COL)), 1.0, 6.0, ((0, 4), (1, 2), (2, 4)))
    potential = jnp.clip(2.0 * jax.random.uniform(arg_keys[1], (ELEMS, E, E * E), jnp.float32) ** level_of(arg_keys[1], (ELEMS, E, E * E), ((0, 4),), -0.2, 0.2), 0.0, 2.0).astype(jnp.bfloat16)
    return {"basis_seed": basis_seed, "potential": potential}


filter_center = 5.5
filter_half = 4.5
penalty = 2.0


def operation_kinds():
    step_kinds = []
    for pass_index in range(PASSES):
        step_kinds = step_kinds + ["first"] + ["later"] * (DEG - 1)
    return step_kinds + ["plain"]


def second_diff(field_cells, axis, stride):
    return (-jnp.roll(field_cells, 2 * stride, axis) + 16.0 * jnp.roll(field_cells, stride, axis) - 30.0 * field_cells + 16.0 * jnp.roll(field_cells, -stride, axis) - jnp.roll(field_cells, -2 * stride, axis)) / 12.0


def apply_box(field_cells, pot_cells, stride):
    laplace = second_diff(field_cells, 0, 1) + second_diff(field_cells, 1, 1) + second_diff(field_cells, 3, stride)
    return -0.5 * laplace + pot_cells * field_cells


def filter_box(seed_box, pot_cells, stride):
    current = seed_box.astype(jnp.float32)
    previous = current
    for step_kind in operation_kinds():
        if step_kind == "plain":
            basis_box = current.astype(jnp.bfloat16)
            rounded = lax.optimization_barrier(basis_box).astype(jnp.float32)
            imaged = apply_box(rounded, pot_cells, stride).astype(jnp.bfloat16)
            return basis_box, imaged
        applied = apply_box(current, pot_cells, stride)
        if step_kind == "first":
            fresh_iter = (applied - filter_center * current) / filter_half
        else:
            fresh_iter = (2.0 / filter_half) * (applied - filter_center * current) - previous
        previous, current = current, fresh_iter


def slope_of(upper_layer, lower_layer):
    return (upper_layer.astype(jnp.float32) - lower_layer.astype(jnp.float32)).astype(jnp.bfloat16)


def cross_sum(left_side, right_side):
    return jnp.einsum("ecp,ecq->epq", left_side.astype(jnp.float32), right_side.astype(jnp.float32), precision=lax.Precision.HIGHEST)


def face_block(face_rows, base):
    top_trace = face_rows[:, base]
    top_slope = face_rows[:, base + 1]
    bottom_trace = face_rows[:, base + 2]
    bottom_slope = face_rows[:, base + 3]
    return penalty * (cross_sum(top_trace, top_trace) + cross_sum(bottom_trace, bottom_trace)) - 0.25 * (cross_sum(top_slope, top_trace) + cross_sum(top_trace, top_slope)) + 0.25 * (cross_sum(bottom_slope, bottom_trace) + cross_sum(bottom_trace, bottom_slope))


def couple_block(top_trace, top_slope, next_bottom, next_slope):
    return 0.25 * cross_sum(top_slope, next_bottom) - 0.25 * cross_sum(top_trace, next_slope) - penalty * cross_sum(top_trace, next_bottom)


def reference(basis_seed, potential):
    width_dev = NB // N_COL

    def element_terms(element):
        pot_box = lax.dynamic_index_in_dim(potential, element, 0, keepdims=False).astype(jnp.float32).reshape(E, E, E)
        pot_cells = jnp.repeat(pot_box, width_dev, axis=2)[:, :, None, :]
        seed_box = jnp.moveaxis(lax.dynamic_index_in_dim(basis_seed, element, 0, keepdims=False), 1, 2)
        basis_box, image_box = filter_box(seed_box, pot_cells, width_dev)
        basis_cells = basis_box.reshape(E, E, N_COL, E, width_dev)
        image_cells = image_box.reshape(E, E, N_COL, E, width_dev)

        def core_rows(values):
            return values[:C, :C, :, :C].transpose(0, 1, 3, 2, 4).reshape(C * C * C, NB)

        volume = jnp.dot(core_rows(basis_cells).T, core_rows(image_cells), preferred_element_type=jnp.float32)

        def y_face(layer_index):
            return basis_cells[:C, :C, :, layer_index].reshape(C * C, NB)

        def z_face(layer_index):
            return basis_cells[:C, layer_index, :, :C].transpose(0, 2, 1, 3).reshape(C * C, NB)

        traces = []
        for face_of in (y_face, z_face):
            top_trace = face_of(C - 1)
            bottom_trace = face_of(0)
            traces = traces + [top_trace, slope_of(top_trace, face_of(C - 2)), bottom_trace, slope_of(face_of(1), bottom_trace)]
        return volume, jnp.stack(traces)

    elements = jnp.arange(ELEMS, dtype=jnp.int32)
    volumes, face_rows = lax.map(element_terms, elements)
    side_next = jnp.take(face_rows, elements ^ 1, axis=0)
    end_next = jnp.take(face_rows, (elements + 2) % ELEMS, axis=0)
    vol_weight = 1.0 / (C * C * C)
    face_weight = 1.0 / (C * C)
    diag_blocks = vol_weight * volumes + face_weight * (face_block(face_rows, 0) + face_block(face_rows, 4))
    coupling_blocks = face_weight * jnp.stack([couple_block(face_rows[:, 0], face_rows[:, 1], side_next[:, 2], side_next[:, 3]), couple_block(face_rows[:, 4], face_rows[:, 5], end_next[:, 6], end_next[:, 7])], 1)
    return diag_blocks, coupling_blocks
```

```python
import functools

import jax
import jax.numpy as jnp
from jax import lax
from jax.experimental import pallas as pl
from jax.experimental.pallas import tpu as pltpu
from jax.sharding import PartitionSpec as P

C = 12
DEG = 4
PASSES = 2
CENTER = 5.5
HALF = 4.5

F32 = jnp.float32
BF16 = jnp.bfloat16
MESH = pl.DeviceIdType.MESH
NT = (((1,), (1,)), ((), ()))


def iota(shape, dim):
    return lax.broadcasted_iota(jnp.int32, shape, dim)


def onehot(cond, value=1.0):
    return jnp.where(cond, value, 0.0)


def dot(a, b):
    return jnp.dot(a, b, preferred_element_type=F32)


def split(a):
    hi = a.astype(BF16)
    return hi, (a - hi.astype(F32)).astype(BF16)


def dot_split(a, b):
    hi, lo = split(a)
    return dot(hi, b) + dot(lo, b)


def swap_halves(a):
    return pltpu.roll(a.reshape(-1, 8, a.shape[-1]), 4, 1).reshape(a.shape)


def kernel(n_elem, n_col, n_pole, seed_ref, pot_ref, diag_ref, coup_ref,
           xsend, xrecv, lsend, lrecv, wsend, wrecv, ysend, yrecv, zsend, zrecv,
           bsend, brecv, send_sem, recv_sem):
    _, rows_dev, _, ext, lanes = seed_ref.shape
    width = lanes // ext
    part = width // 2
    groups = part // 4
    half = ext // 2
    cells = ext * ext
    own_cells = rows_dev * ext
    rows = half * groups * 8
    packed = (C // 2) * groups * 8
    pair = 2 * groups * 8
    blocks = packed // 16

    e = lax.axis_index("elem")
    c = lax.axis_index("col")
    p = lax.axis_index("pole")
    h = lax.rem(p, 2)
    mate = p + 1 - 2 * h
    far = lax.rem(c + n_col // 2, n_col)
    near = c + 1 - 2 * lax.rem(c, 2)
    other = 1 - h
    side_e = e + 1 - 2 * lax.rem(e, 2)
    prev_e = lax.rem(e + n_elem - 2, n_elem)
    next_e = lax.rem(e + 2, n_elem)
    peers = [(e, c, mate), (e, near, p), (e, near, mate)]
    turns = [lax.rem(p + k, n_pole) for k in range(1, n_pole)]
    turned = [lax.rem(p + n_pole - k, n_pole) for k in range(1, n_pole)]

    barrier = pltpu.get_barrier_semaphore()
    greet = peers[1:] + [(e, c, turn) for turn in turns]
    greet += [(e, far, p), (side_e, c, p), (side_e, far, p),
              (prev_e, c, p), (prev_e, far, p), (next_e, c, p), (next_e, far, p)]
    for device in greet:
        pl.semaphore_signal(barrier, inc=1, device_id=device, device_id_type=MESH)

    def remote(src, dst, sem, device):
        return pltpu.make_async_remote_copy(
            src_ref=src, dst_ref=dst, send_sem=send_sem.at[sem], recv_sem=recv_sem.at[sem],
            device_id=device, device_id_type=MESH)

    seed = seed_ref[0, :, 0].reshape(own_cells, lanes)
    sel_shape = (half, groups, 8, lanes)
    row_s = iota(sel_shape, 2)
    row_col = (iota(sel_shape, 0) * width + iota(sel_shape, 1) * 4 + (row_s & 3)
               + (row_s >> 2) * (half * width))
    lane = iota(sel_shape, 3)

    def pick(which):
        sel = onehot(lane == row_col + which * part).reshape(rows, lanes).astype(BF16)
        return lax.dot_general(sel, seed, NT, preferred_element_type=F32)

    for k, turn in enumerate(turns):
        xsend[k] = pick(lax.rem(turn, 2)).astype(BF16)
    pl.semaphore_wait(barrier, len(greet))
    first_copies = [remote(xsend.at[k], xrecv.at[k], 12 + k, (e, c, turn))
                    for k, turn in enumerate(turns)]
    for copy in first_copies:
        copy.start()
    own = pick(h)

    i0, i1 = iota((cells, cells), 0), iota((cells, cells), 1)
    same_x = (i0 // ext) == (i1 // ext)
    same_z = (i0 & (ext - 1)) == (i1 & (ext - 1))
    dz = (i0 - i1) & (ext - 1)
    dx = ((i0 - i1) // ext) & (ext - 1)

    def ring(d):
        return jnp.where((d == 1) | (d == ext - 1), -16.0,
                         jnp.where((d == 2) | (d == ext - 2), 1.0,
                                   jnp.where(d == 0, 30.0, 0.0)))

    stencil = jnp.where(same_x, ring(dz), 0.0) + jnp.where(same_z, ring(dx), 0.0)
    z0, z1 = i0 & (ext - 1), i1 & (ext - 1)
    corner = ((z0 == 0) & (z1 == 0)) | ((z0 == C - 1) & (z1 == C - 1))
    edge = (((z0 + z1) == 1) | ((z0 + z1) == 2 * C - 3)) & (
        (z0 - z1 == 1) | (z1 - z0 == 1))
    face = 24.0 * C
    stencil_w = stencil + jnp.where(same_x & corner, 1.5 * face, 0.0) + jnp.where(
        same_x & edge, 0.25 * face, 0.0)
    stencil = stencil.astype(BF16)
    stencil_w = stencil_w.astype(BF16)

    r0, l0 = iota((cells, 128), 0), iota((cells, 128), 1)
    rx, rz = r0 // ext, r0 & (ext - 1)
    core = (rx < C) & (rz < C)
    target = (C - 1 - rz) * C + rx
    to_main = onehot(core & (l0 == target)).astype(BF16)
    to_rest = onehot(core & ((l0 & 15) == target - 128)).astype(BF16)
    l32 = l0 & 31
    to_next = (onehot((rx < C) & (rz == 0) & (l32 == rx), -1.5)
               + onehot((rx < C) & (rz == 1) & (l32 == rx), -0.25)
               + onehot((rx < C) & (rz == 0) & (l32 == C + rx), -0.25)).astype(BF16)
    rep0, rep1 = iota((128, 128), 0), iota((128, 128), 1)
    to_top = onehot((rep0 < 2 * C) & ((rep1 & 31) == rep0)).astype(BF16)

    pot = pot_ref[0].astype(F32)
    p_shape = (ext, ext, cells)
    pot_z = jnp.where(iota(p_shape, 2) // ext == iota(p_shape, 1), pot[:, None, :], 0.0)
    v_shape = (half, 8, cells)
    v_sel = onehot((iota(v_shape, 2) & (ext - 1)) == iota(v_shape, 0)
                   + (iota(v_shape, 1) >> 2) * half).reshape(half * 8, cells).astype(BF16)
    pot_y = lax.dot_general(v_sel, pot_z.reshape(cells, cells).astype(BF16), NT,
                            preferred_element_type=F32).reshape(half, 1, 8, cells)
    scaled = (2.0 / HALF) * (pot_y + (1.25 - CENTER))
    scaled24 = 24.0 * pot_y + 30.0
    four_d = (half, groups, 8, cells)

    for copy in first_copies:
        copy.wait()
    pieces = []
    for source in range(n_pole):
        piece = own
        for k, turn in enumerate(turned):
            piece = jnp.where(turn == source, xrecv[k].astype(F32), piece)
        pieces.append(piece)
    start = jnp.concatenate(pieces, axis=1)

    def rows_part(f4):
        ext_f = jnp.concatenate([swap_halves(f4[half - 2:]), f4, swap_halves(f4[:2])], axis=0)
        return (ext_f[:half] + ext_f[4:]) - 16.0 * (ext_f[1:half + 1] + ext_f[3:half + 3])

    current = start.reshape(four_d)
    previous = None
    scale = 2.0 / (HALF * 24.0)
    for _ in range(PASSES):
        for k in range(DEG):
            f4 = current
            mixed = dot_split(f4.reshape(rows, cells), stencil).reshape(four_d)
            fresh = scale * (mixed + rows_part(f4)) + scaled * f4
            fresh = 0.5 * fresh if k == 0 else fresh - previous
            previous, current = f4, fresh

    basis = current.reshape(rows, cells).astype(BF16)
    basis4 = basis.astype(F32).reshape(four_d)
    upper = iota((1, groups, 8, cells), 2) >= 4

    def pack_rows(a4):
        rest = jnp.where(upper, swap_halves(a4[6:8]), a4[4:6])
        return jnp.concatenate([a4[:4], rest], axis=0).reshape(packed, cells).astype(BF16)

    def pack_blocks(a, wide):
        count = 128 // wide
        n = a.shape[0] // 16
        group = iota((16, 128), 1) // wide
        out = []
        for base in range(0, n, count):
            total = None
            for b in range(base, min(base + count, n)):
                term = jnp.where(group == b - base, a[b * 16:(b + 1) * 16], 0.0)
                total = term if total is None else total + term
            out.append(total)
        return jnp.concatenate(out, axis=0).astype(BF16)

    def unpack_blocks(tiles, n, wide):
        count = 128 // wide
        group = iota((16, 128), 1) // wide
        out = []
        for b in range(n):
            tile = tiles[(b // count) * 16:(b // count + 1) * 16].astype(F32)
            out.append(jnp.where(group == b % count, tile, 0.0))
        return jnp.concatenate(out, axis=0).astype(BF16)

    core_basis = pack_rows(basis4)
    left_main = dot(core_basis, to_main).astype(BF16)
    left_rest = dot(core_basis, to_rest)
    lsend[:packed] = left_main
    lsend[packed:] = pack_blocks(left_rest, 16)
    copies = [remote(lsend, lrecv.at[k], 1 + k, peers[k]) for k in range(3)]
    for copy in copies:
        copy.start()

    low_n = basis4[0:1] * -1.5 + basis4[1:2] * -0.25
    low_s = basis4[0:1] * -0.25
    y_rows = jnp.concatenate([jnp.where(upper, swap_halves(low_s), 0.0),
                              jnp.where(upper, swap_halves(low_n), 0.0)], axis=0)
    y_rows = y_rows.reshape(pair, cells).astype(BF16)
    ysend[:pair] = dot(y_rows, to_main).astype(BF16)
    ysend[pair:] = pack_blocks(dot(y_rows, to_rest), 16)
    zsend[...] = pack_blocks(dot(core_basis, to_next), 32)
    bottom_copies = [remote(ysend, yrecv.at[1], 5, (side_e, far, p)),
                     remote(zsend, zrecv.at[1], 7, (prev_e, far, p)),
                     remote(ysend, yrecv.at[0], 6, (side_e, c, p)),
                     remote(zsend, zrecv.at[0], 8, (prev_e, c, p))]

    image = dot(basis, stencil_w).reshape(four_d) + rows_part(basis4) + scaled24 * basis4
    low, high = jnp.logical_not(upper), upper
    image = jnp.concatenate([
        image[0:1] + jnp.where(low, face * (1.5 * basis4[0:1] + 0.25 * basis4[1:2]), 0.0),
        image[1:2] + jnp.where(low, face * 0.25 * basis4[0:1], 0.0),
        image[2:3] + jnp.where(high, face * 0.25 * basis4[3:4], 0.0),
        image[3:4] + jnp.where(high, face * (1.5 * basis4[3:4] + 0.25 * basis4[2:3]), 0.0),
        image[4:]], axis=0)
    core_image = pack_rows(image)
    right_main = dot(core_image, to_main).astype(BF16)
    right_rest = pack_blocks(dot(core_image, to_rest), 16)
    wsend[:packed] = right_main
    wsend[packed:] = right_rest
    w_copy = remote(wsend, wrecv, 4, (e, far, p))
    w_copy.start()
    for copy in bottom_copies:
        copy.start()

    m0, m1 = iota((4 * pair, 2 * pair), 0), iota((4 * pair, 2 * pair), 1)
    per = groups * 8
    same_y = ((m0 // per) & 1 == (m1 // per) & 1) & ((m0 >> 2) & 1 == (m1 >> 2) & 1)
    q0, q1 = iota((2 * pair, 128), 0), iota((2 * pair, 128), 1)
    q_lane = (q0 // pair) * part + ((q0 % per) // 8) * 4 + (q0 & 3)
    to_q = [onehot(q1 == q_lane + 32 * k).astype(BF16) for k in range(3)]
    s0, s1 = iota((width, 2 * pair), 0), iota((width, 2 * pair), 1)
    slot_half = jnp.where(s1 // pair == 0, h, other)
    to_p = onehot(s0 == slot_half * part + ((s1 % per) // 8) * 4 + (s1 & 3)).astype(BF16)
    o0, o1 = iota((128, 384), 0), iota((128, 384), 1)
    o_q = o0 & 31
    o_slot = o_q >= part
    o_fit = (o_q < 2 * part) & ((o0 // 32) == (o1 // 128))

    def to_out(col, half_of):
        there = jnp.where(o_slot, lax.rem(col + n_col // 2, n_col) * width - part, col * width)
        return onehot(o_fit & ((o1 & 127) == there + half_of * part + o_q)).astype(BF16)

    outs = jnp.concatenate([to_out(c, h), to_out(c, other), to_out(near, h),
                            to_out(near, other)], axis=0)

    def full(main, rest):
        return jnp.concatenate([main, unpack_blocks(rest, main.shape[0] // 16, 16)], axis=1)

    own_right = full(right_main, right_rest)

    for copy in copies:
        copy.wait()
    fold0, fold1 = iota((128, 128), 0), iota((128, 128), 1)
    spread = onehot((fold0 & 15) == (fold1 & 15)).astype(BF16)
    lefts = [jnp.concatenate([left_main, left_rest.astype(BF16)], axis=1)]
    for k in range(3):
        main = lrecv[k, :packed]
        rest = unpack_blocks(lrecv[k, packed:], blocks, 16)
        lefts.append(jnp.concatenate([main, dot(rest, spread).astype(BF16)], axis=1))
    tops = [dot(left[:, :128], to_top).astype(BF16) for left in lefts]

    def stack(parts, t):
        return jnp.concatenate([a[t * pair:(t + 1) * pair] for a in parts], axis=0)

    def nt(a, b):
        return lax.dot_general(a, b, NT, preferred_element_type=F32)

    for copy in bottom_copies:
        copy.wait()
    y_right = jnp.concatenate([full(yrecv[k, :pair], yrecv[k, pair:]) for k in range(2)], axis=0)
    z_right = [unpack_blocks(zrecv[k], blocks, 32) for k in range(2)]
    left_t = [stack(lefts, t) for t in range(3)]
    y_sum = nt(left_t[1], y_right)
    z_sum = sum(nt(stack(tops, t), stack(z_right, t)) for t in range(3))
    w_copy.wait()
    rights = [own_right, full(wrecv[:packed], wrecv[packed:])]
    d_sum = sum(nt(left_t[t], stack(rights, t)) for t in range(3))

    weights = [1.0 / (24.0 * C * C * C), 1.0 / (C * C), 1.0 / (C * C)]
    packed_q = sum(dot_split(jnp.where(same_y, total * weight, 0.0), sel)
                   for total, weight, sel in zip([d_sum, y_sum, z_sum], weights, to_q))
    hi, lo = split(packed_q)
    bsend[1] = dot(to_p, hi[2 * pair:]) + dot(to_p, lo[2 * pair:])
    mine = dot(to_p, hi[:2 * pair]) + dot(to_p, lo[:2 * pair])
    bsend[0] = mine
    last = [remote(bsend.at[min(k, 1)], brecv.at[k], 9 + k, peers[k]) for k in range(3)]
    for copy in last:
        copy.start()
    for copy in last:
        copy.wait()
    every = jnp.concatenate([mine, brecv[0], brecv[1], brecv[2]], axis=1)
    result = dot_split(every, outs)
    n_all = n_col * width
    diag_ref[0] = result[:, :n_all]
    coup_ref[0, 0] = result[:, 128:128 + n_all]
    coup_ref[0, 1] = result[:, 256:256 + n_all]


def solution(mesh):
    sizes = dict(mesh.shape)
    n_elem, n_col, n_pole = sizes["elem"], sizes["col"], sizes["pole"]
    assert n_pole % 2 == 0 and n_col == 4

    def local(basis_seed, potential):
        _, _, _, ext, lanes = basis_seed.shape
        width = lanes // ext
        part = width // 2
        rows = ext * part
        packed = C * part
        pair = 4 * part
        tail = 16 * (-(-packed // 128))
        n_all = width * n_col
        own_cells = basis_seed.shape[1] * ext
        turns = n_pole - 1
        vm = pltpu.VMEM
        return pl.pallas_call(
            functools.partial(kernel, n_elem, n_col, n_pole),
            out_shape=(jax.ShapeDtypeStruct((1, width, n_all), F32),
                       jax.ShapeDtypeStruct((1, 2, width, n_all), F32)),
            in_specs=[pl.BlockSpec(memory_space=pltpu.VMEM)] * 2,
            out_specs=(pl.BlockSpec(memory_space=pltpu.VMEM),) * 2,
            scratch_shapes=[
                vm((turns, rows, own_cells), BF16), vm((turns, rows, own_cells), BF16),
                vm((packed + tail, 128), BF16), vm((3, packed + tail, 128), BF16),
                vm((packed + tail, 128), BF16), vm((packed + tail, 128), BF16),
                vm((pair + 16, 128), BF16), vm((2, pair + 16, 128), BF16),
                vm((48, 128), BF16), vm((2, 48, 128), BF16),
                vm((2, width, 128), F32), vm((3, width, 128), F32),
                pltpu.SemaphoreType.DMA((12 + turns,)), pltpu.SemaphoreType.DMA((12 + turns,)),
            ],
            compiler_params=pltpu.CompilerParams(
                collective_id=0, has_side_effects=True, vmem_limit_bytes=48 * 1024 * 1024),
        )(basis_seed, potential)

    return jax.shard_map(
        local,
        mesh=mesh,
        in_specs=(P("elem", "pole", "col", None, None), P("elem", None, None)),
        out_specs=(P("elem", "col", None), P("elem", None, "col", None)),
        check_vma=False,
    )
```

```python
import functools

import jax
import jax.numpy as jnp
from jax import lax
from jax.experimental import pallas as pl
from jax.experimental.pallas import tpu as pltpu
from jax.sharding import PartitionSpec as P

C = 12
DEG = 4
PASSES = 2
CENTER = 5.5
HALF = 4.5

F32 = jnp.float32
BF16 = jnp.bfloat16
MESH = pl.DeviceIdType.MESH
NT = (((1,), (1,)), ((), ()))


def iota(shape, dim):
    return lax.broadcasted_iota(jnp.int32, shape, dim)


def onehot(cond, value=1.0):
    return jnp.where(cond, value, 0.0)


def dot(a, b):
    return jnp.dot(a, b, preferred_element_type=F32)


def split(a):
    hi = a.astype(BF16)
    return hi, (a - hi.astype(F32)).astype(BF16)


def dot_split(a, b):
    hi, lo = split(a)
    return dot(hi, b) + dot(lo, b)


def swap_halves(a):
    return pltpu.roll(a.reshape(-1, 8, a.shape[-1]), 4, 1).reshape(a.shape)


def kernel(n_elem, n_col, n_pole, seed_ref, pot_ref, out_ref,
           xsend, xrecv, lsend, lrecv, wsend, wrecv, ysend, yrecv, zsend, zrecv,
           bsend, brecv, seed_here, pot_here, sel_ref, local_sem, send_sem, recv_sem):
    seed_copy = pltpu.make_async_copy(seed_ref, seed_here, local_sem.at[0])
    pot_copy = pltpu.make_async_copy(pot_ref, pot_here, local_sem.at[1])
    seed_copy.start()
    pot_copy.start()
    _, rows_dev, _, ext, lanes = seed_ref.shape
    width = lanes // ext
    part = width // 2
    groups = part // 4
    half = ext // 2
    cells = ext * ext
    own_cells = rows_dev * ext
    rows = half * groups * 8
    packed = (C // 2) * groups * 8
    pair = 2 * groups * 8
    blocks = packed // 16

    e = lax.axis_index("elem")
    c = lax.axis_index("col")
    p = lax.axis_index("pole")
    h = lax.rem(p, 2)
    mate = p + 1 - 2 * h
    far = lax.rem(c + n_col // 2, n_col)
    near = c + 1 - 2 * lax.rem(c, 2)
    other = 1 - h
    side_e = e + 1 - 2 * lax.rem(e, 2)
    prev_e = lax.rem(e + n_elem - 2, n_elem)
    next_e = lax.rem(e + 2, n_elem)
    peers = [(e, c, mate), (e, near, p), (e, near, mate)]
    turns = [lax.rem(p + k, n_pole) for k in range(1, n_pole)]
    turned = [lax.rem(p + n_pole - k, n_pole) for k in range(1, n_pole)]

    barrier = pltpu.get_barrier_semaphore()
    greet = peers[1:] + [(e, c, turn) for turn in turns]
    greet += [(e, far, p), (side_e, c, p), (side_e, far, p),
              (prev_e, c, p), (prev_e, far, p), (next_e, c, p), (next_e, far, p)]
    for device in greet:
        pl.semaphore_signal(barrier, inc=1, device_id=device, device_id_type=MESH)

    def remote(src, dst, sem, device):
        return pltpu.make_async_remote_copy(
            src_ref=src, dst_ref=dst, send_sem=send_sem.at[sem], recv_sem=recv_sem.at[sem],
            device_id=device, device_id_type=MESH)

    sel_shape = (half, groups, 8, lanes)
    row_s = iota(sel_shape, 2)
    row_col = (iota(sel_shape, 0) * width + iota(sel_shape, 1) * 4 + (row_s & 3)
               + (row_s >> 2) * (half * width))
    lane = iota(sel_shape, 3)

    def fill(slot, which):
        sel_ref[slot] = onehot(lane == row_col + which * part).reshape(rows, lanes).astype(BF16)

    def pick(slot, seed):
        return lax.dot_general(sel_ref[slot], seed, NT, preferred_element_type=F32)

    fill(0, other)
    fill(1, h)
    seed_copy.wait()
    seed = seed_here[0, :, 0].reshape(own_cells, lanes)
    for k, turn in enumerate(turns):
        xsend[k] = pick(k % 2, seed).astype(BF16)
    pl.semaphore_wait(barrier, len(greet))
    first_copies = [remote(xsend.at[k], xrecv.at[k], 12 + k, (e, c, turn))
                    for k, turn in enumerate(turns)]
    for copy in first_copies:
        copy.start()
    own = pick(1, seed)

    i0, i1 = iota((cells, cells), 0), iota((cells, cells), 1)
    same_x = (i0 // ext) == (i1 // ext)
    same_z = (i0 & (ext - 1)) == (i1 & (ext - 1))
    dz = (i0 - i1) & (ext - 1)
    dx = ((i0 - i1) // ext) & (ext - 1)

    def ring(d):
        return jnp.where((d == 1) | (d == ext - 1), -16.0,
                         jnp.where((d == 2) | (d == ext - 2), 1.0,
                                   jnp.where(d == 0, 30.0, 0.0)))

    stencil = jnp.where(same_x, ring(dz), 0.0) + jnp.where(same_z, ring(dx), 0.0)
    z0, z1 = i0 & (ext - 1), i1 & (ext - 1)
    corner = ((z0 == 0) & (z1 == 0)) | ((z0 == C - 1) & (z1 == C - 1))
    edge = (((z0 + z1) == 1) | ((z0 + z1) == 2 * C - 3)) & (
        (z0 - z1 == 1) | (z1 - z0 == 1))
    face = 24.0 * C
    stencil_w = stencil + jnp.where(same_x & corner, 1.5 * face, 0.0) + jnp.where(
        same_x & edge, 0.25 * face, 0.0)
    stencil = stencil.astype(BF16)
    stencil_w = stencil_w.astype(BF16)

    r0, l0 = iota((cells, 128), 0), iota((cells, 128), 1)
    rx, rz = r0 // ext, r0 & (ext - 1)
    core = (rx < C) & (rz < C)
    target = (C - 1 - rz) * C + rx
    to_main = onehot(core & (l0 == target)).astype(BF16)
    to_rest = onehot(core & ((l0 & 15) == target - 128)).astype(BF16)
    l32 = l0 & 31
    to_next = (onehot((rx < C) & (rz == 0) & (l32 == rx), -1.5)
               + onehot((rx < C) & (rz == 1) & (l32 == rx), -0.25)
               + onehot((rx < C) & (rz == 0) & (l32 == C + rx), -0.25)).astype(BF16)
    rep0, rep1 = iota((128, 128), 0), iota((128, 128), 1)
    to_top = onehot((rep0 < 2 * C) & ((rep1 & 31) == rep0)).astype(BF16)

    pot_copy.wait()
    pot = pot_here[0].astype(F32)
    p_shape = (ext, ext, cells)
    pot_z = jnp.where(iota(p_shape, 2) // ext == iota(p_shape, 1), pot[:, None, :], 0.0)
    v_shape = (half, 8, cells)
    v_sel = onehot((iota(v_shape, 2) & (ext - 1)) == iota(v_shape, 0)
                   + (iota(v_shape, 1) >> 2) * half).reshape(half * 8, cells).astype(BF16)
    pot_y = lax.dot_general(v_sel, pot_z.reshape(cells, cells).astype(BF16), NT,
                            preferred_element_type=F32).reshape(half, 1, 8, cells)
    scaled = (2.0 / HALF) * (pot_y + (1.25 - CENTER))
    scaled24 = 24.0 * pot_y + 30.0
    four_d = (half, groups, 8, cells)

    for copy in first_copies:
        copy.wait()
    pieces = []
    for source in range(n_pole):
        piece = own
        for k, turn in enumerate(turned):
            piece = jnp.where(turn == source, xrecv[k].astype(F32), piece)
        pieces.append(piece)
    start = jnp.concatenate(pieces, axis=1)

    def rows_part(f4):
        ext_f = jnp.concatenate([swap_halves(f4[half - 2:]), f4, swap_halves(f4[:2])], axis=0)
        return (ext_f[:half] + ext_f[4:]) - 16.0 * (ext_f[1:half + 1] + ext_f[3:half + 3])

    current = start.reshape(four_d)
    previous = None
    scale = 2.0 / (HALF * 24.0)
    for _ in range(PASSES):
        for k in range(DEG):
            f4 = current
            mixed = dot_split(f4.reshape(rows, cells), stencil).reshape(four_d)
            fresh = scale * (mixed + rows_part(f4)) + scaled * f4
            fresh = 0.5 * fresh if k == 0 else fresh - previous
            previous, current = f4, fresh

    basis = current.reshape(rows, cells).astype(BF16)
    basis4 = basis.astype(F32).reshape(four_d)
    upper = iota((1, groups, 8, cells), 2) >= 4

    def pack_rows(a4):
        rest = jnp.where(upper, swap_halves(a4[6:8]), a4[4:6])
        return jnp.concatenate([a4[:4], rest], axis=0).reshape(packed, cells).astype(BF16)

    def pack_blocks(a, wide):
        count = 128 // wide
        n = a.shape[0] // 16
        group = iota((16, 128), 1) // wide
        out = []
        for base in range(0, n, count):
            total = None
            for b in range(base, min(base + count, n)):
                term = jnp.where(group == b - base, a[b * 16:(b + 1) * 16], 0.0)
                total = term if total is None else total + term
            out.append(total)
        return jnp.concatenate(out, axis=0).astype(BF16)

    def unpack_blocks(tiles, n, wide):
        count = 128 // wide
        group = iota((16, 128), 1) // wide
        out = []
        for b in range(n):
            tile = tiles[(b // count) * 16:(b // count + 1) * 16].astype(F32)
            out.append(jnp.where(group == b % count, tile, 0.0))
        return jnp.concatenate(out, axis=0).astype(BF16)

    core_basis = pack_rows(basis4)
    left_main = dot(core_basis, to_main).astype(BF16)
    left_rest = dot(core_basis, to_rest)
    lsend[:packed] = left_main
    lsend[packed:] = pack_blocks(left_rest, 16)
    copies = [remote(lsend, lrecv.at[k], 1 + k, peers[k]) for k in range(3)]
    for copy in copies:
        copy.start()

    low_n = basis4[0:1] * -1.5 + basis4[1:2] * -0.25
    low_s = basis4[0:1] * -0.25
    y_rows = jnp.concatenate([jnp.where(upper, swap_halves(low_s), 0.0),
                              jnp.where(upper, swap_halves(low_n), 0.0)], axis=0)
    y_rows = y_rows.reshape(pair, cells).astype(BF16)
    ysend[:pair] = dot(y_rows, to_main).astype(BF16)
    ysend[pair:] = pack_blocks(dot(y_rows, to_rest), 16)
    zsend[...] = pack_blocks(dot(core_basis, to_next), 32)
    bottom_copies = [remote(ysend, yrecv.at[1], 5, (side_e, far, p)),
                     remote(zsend, zrecv.at[1], 7, (prev_e, far, p)),
                     remote(ysend, yrecv.at[0], 6, (side_e, c, p)),
                     remote(zsend, zrecv.at[0], 8, (prev_e, c, p))]

    image = dot(basis, stencil_w).reshape(four_d) + rows_part(basis4) + scaled24 * basis4
    low, high = jnp.logical_not(upper), upper
    image = jnp.concatenate([
        image[0:1] + jnp.where(low, face * (1.5 * basis4[0:1] + 0.25 * basis4[1:2]), 0.0),
        image[1:2] + jnp.where(low, face * 0.25 * basis4[0:1], 0.0),
        image[2:3] + jnp.where(high, face * 0.25 * basis4[3:4], 0.0),
        image[3:4] + jnp.where(high, face * (1.5 * basis4[3:4] + 0.25 * basis4[2:3]), 0.0),
        image[4:]], axis=0)
    core_image = pack_rows(image)
    right_main = dot(core_image, to_main).astype(BF16)
    right_rest = pack_blocks(dot(core_image, to_rest), 16)
    wsend[:packed] = right_main
    wsend[packed:] = right_rest
    w_copy = remote(wsend, wrecv, 4, (e, far, p))
    w_copy.start()
    for copy in bottom_copies:
        copy.start()

    m0, m1 = iota((4 * pair, 2 * pair), 0), iota((4 * pair, 2 * pair), 1)
    per = groups * 8
    same_y = ((m0 // per) & 1 == (m1 // per) & 1) & ((m0 >> 2) & 1 == (m1 >> 2) & 1)
    q0, q1 = iota((2 * pair, 128), 0), iota((2 * pair, 128), 1)
    q_lane = (q0 // pair) * part + ((q0 % per) // 8) * 4 + (q0 & 3)
    to_q = [onehot(q1 == q_lane + 32 * k).astype(BF16) for k in range(3)]
    s0, s1 = iota((width, 2 * pair), 0), iota((width, 2 * pair), 1)
    slot_half = jnp.where(s1 // pair == 0, h, other)
    to_p = onehot(s0 == slot_half * part + ((s1 % per) // 8) * 4 + (s1 & 3)).astype(BF16)
    o0, o1 = iota((128, 384), 0), iota((128, 384), 1)
    o_q = o0 & 31
    o_slot = o_q >= part
    o_fit = (o_q < 2 * part) & ((o0 // 32) == (o1 // 128))

    def to_out(col, half_of):
        there = jnp.where(o_slot, lax.rem(col + n_col // 2, n_col) * width - part, col * width)
        return onehot(o_fit & ((o1 & 127) == there + half_of * part + o_q)).astype(BF16)

    outs = jnp.concatenate([to_out(c, h), to_out(c, other), to_out(near, h),
                            to_out(near, other)], axis=0)

    def full(main, rest):
        return jnp.concatenate([main, unpack_blocks(rest, main.shape[0] // 16, 16)], axis=1)

    own_right = full(right_main, right_rest)

    for copy in copies:
        copy.wait()
    fold0, fold1 = iota((128, 128), 0), iota((128, 128), 1)
    spread = onehot((fold0 & 15) == (fold1 & 15)).astype(BF16)
    lefts = [jnp.concatenate([left_main, left_rest.astype(BF16)], axis=1)]
    for k in range(3):
        main = lrecv[k, :packed]
        rest = unpack_blocks(lrecv[k, packed:], blocks, 16)
        lefts.append(jnp.concatenate([main, dot(rest, spread).astype(BF16)], axis=1))
    tops = [dot(left[:, :128], to_top).astype(BF16) for left in lefts]

    def stack(parts, t):
        return jnp.concatenate([a[t * pair:(t + 1) * pair] for a in parts], axis=0)

    def nt(a, b):
        return lax.dot_general(a, b, NT, preferred_element_type=F32)

    for copy in bottom_copies:
        copy.wait()
    y_right = jnp.concatenate([full(yrecv[k, :pair], yrecv[k, pair:]) for k in range(2)], axis=0)
    z_right = [unpack_blocks(zrecv[k], blocks, 32) for k in range(2)]
    left_t = [stack(lefts, t) for t in range(3)]
    y_sum = nt(left_t[1], y_right)
    z_sum = sum(nt(stack(tops, t), stack(z_right, t)) for t in range(3))
    near_sum = sum(nt(left_t[t], own_right[t * pair:(t + 1) * pair]) for t in range(3))

    def to_columns(total, mask, weight, sel):
        return dot_split(jnp.where(mask, total * weight, 0.0), sel)

    vol_weight, face_weight = 1.0 / (24.0 * C * C * C), 1.0 / (C * C)
    same_one = same_y[:, :pair]
    packed_q = (to_columns(y_sum, same_y, face_weight, to_q[1])
                + to_columns(z_sum, same_y, face_weight, to_q[2])
                + to_columns(near_sum, same_one, vol_weight, to_q[0][:pair]))
    w_copy.wait()
    far_right = full(wrecv[:packed], wrecv[packed:])
    far_sum = sum(nt(left_t[t], far_right[t * pair:(t + 1) * pair]) for t in range(3))
    packed_q = packed_q + to_columns(far_sum, same_one, vol_weight, to_q[0][pair:])
    hi, lo = split(packed_q)
    bsend[1] = dot(to_p, hi[2 * pair:]) + dot(to_p, lo[2 * pair:])
    mine = dot(to_p, hi[:2 * pair]) + dot(to_p, lo[:2 * pair])
    bsend[0] = mine
    last = [remote(bsend.at[min(k, 1)], brecv.at[k], 9 + k, peers[k]) for k in range(3)]
    for copy in last:
        copy.start()
    for copy in last:
        copy.wait()
    every = jnp.concatenate([mine, brecv[0], brecv[1], brecv[2]], axis=1)
    out_ref[...] = dot_split(every, outs)


def write_out(all_ref, diag_ref, coup_ref):
    n_all = diag_ref.shape[-1]
    diag_ref[0] = all_ref[:, :n_all]
    coup_ref[0, 0] = all_ref[:, 128:128 + n_all]
    coup_ref[0, 1] = all_ref[:, 256:256 + n_all]


def solution(mesh):
    sizes = dict(mesh.shape)
    n_elem, n_col, n_pole = sizes["elem"], sizes["col"], sizes["pole"]
    assert n_pole % 2 == 0 and n_col == 4

    def local(basis_seed, potential):
        _, _, _, ext, lanes = basis_seed.shape
        width = lanes // ext
        part = width // 2
        rows = ext * part
        packed = C * part
        pair = 4 * part
        tail = 16 * (-(-packed // 128))
        n_all = width * n_col
        own_cells = basis_seed.shape[1] * ext
        turns = n_pole - 1
        vm = pltpu.VMEM
        whole = pl.pallas_call(
            functools.partial(kernel, n_elem, n_col, n_pole),
            out_shape=jax.ShapeDtypeStruct((width, 3 * 128), F32),
            in_specs=[pl.BlockSpec(memory_space=pl.ANY)] * 2,
            out_specs=pl.BlockSpec(memory_space=pltpu.VMEM),
            scratch_shapes=[
                vm((turns, rows, own_cells), BF16), vm((turns, rows, own_cells), BF16),
                vm((packed + tail, 128), BF16), vm((3, packed + tail, 128), BF16),
                vm((packed + tail, 128), BF16), vm((packed + tail, 128), BF16),
                vm((pair + 16, 128), BF16), vm((2, pair + 16, 128), BF16),
                vm((48, 128), BF16), vm((2, 48, 128), BF16),
                vm((2, width, 128), F32), vm((3, width, 128), F32),
                vm(basis_seed.shape, BF16), vm(potential.shape, BF16), vm((2, rows, lanes), BF16), pltpu.SemaphoreType.DMA((2,)),
                pltpu.SemaphoreType.DMA((12 + turns,)), pltpu.SemaphoreType.DMA((12 + turns,)),
            ],
            compiler_params=pltpu.CompilerParams(
                collective_id=0, has_side_effects=True, vmem_limit_bytes=60 * 1024 * 1024),
        )(basis_seed, potential)
        return pl.pallas_call(
            write_out,
            out_shape=(jax.ShapeDtypeStruct((1, width, n_all), F32),
                       jax.ShapeDtypeStruct((1, 2, width, n_all), F32)),
            in_specs=[pl.BlockSpec(memory_space=pltpu.VMEM)],
            out_specs=(pl.BlockSpec(memory_space=pltpu.VMEM),) * 2,
        )(whole)

    return jax.shard_map(
        local,
        mesh=mesh,
        in_specs=(P("elem", "pole", "col", None, None), P("elem", None, None)),
        out_specs=(P("elem", "col", None), P("elem", None, "col", None)),
        check_vma=False,
    )
```
